256 devices in a mesh: tm: 8 (over x, y_lo), space: 32 (over z, y_hi, core).
Axes of the slice: x: 4, y: 4 (y_hi: 2, y_lo: 2; y = y_hi * 2 + y_lo), z: 8, core: 2. Of those that a mesh axis runs over, the one named last changes fastest.
Arguments:
- snapshots: bfloat16 [128, 256, 32768], P('tm', None, 'space'), may hold values from -6 to 6
- weights: float32 [32768], P('space'), may hold values from 1.5258789e-05 to 0.00024414062
Outputs:
- spectra: float32 [128, 128, 2, 128], P('space', 'tm')
The draws below stay inside these ranges and needn't reach their ends.
All inputs are finite; a program needn't handle non-finite values.
Results may differ from the reference program's by a relative error of at most 0.0027.
Values may be sent and summed in bfloat16 or wider, within the bound.
No kernel may reach another device: no remote copies, remote signals or barrier semaphores. Data moves between devices by JAX's collectives and lax.ppermute only.
A program may use at most 192 MiB of HBM per device.

```python
import math
import jax
import jax.numpy as jnp
from jax import lax

NB = 128
NFFT = 256
NF = 128
X_DEV = 1024
XTOT = 32768
N_SPACE = 32


def shard_levels(key, dims, split, low, high):
    loudness, own = 1.0, jax.random.fold_in(key, 6)
    for position, parts in split:
        draws = jnp.exp(jax.random.uniform(jax.random.fold_in(own, position), (parts,), jnp.float32, low / len(split), high / len(split)))
        loudness = loudness * jnp.repeat(draws, dims[position] // parts).reshape([-1 if axis == position else 1 for axis in range(len(dims))])
    return loudness


def noise(own_key, shape, spread, limit, split=(), kind=jnp.bfloat16):
    result = jax.random.normal(own_key, shape, jnp.float32) * spread
    if len(split) > 0:
        result = shard_levels(own_key, shape, split, -0.22, 0.18) * result
    return jnp.clip(result, min=-limit, max=limit).astype(kind)


def setup_inputs(seed: int = 0) -> dict:
    key_of = jax.random.split(jax.random.key(seed), 3)
    snapshots = noise(key_of[0], (NB, NFFT, XTOT), 1.0, 6.0, ((0, 8), (2, 32)))
    weights = jnp.clip(jnp.exp(math.log(0.00024414062) - 2.7725887 * jax.random.uniform(key_of[1], (XTOT,), jnp.float32) ** shard_levels(key_of[1], (XTOT,), ((0, 32),), -0.2, 0.2)), 1.52587890625e-05, 0.00024414062)
    return dict(snapshots=snapshots, weights=weights)


def make_table():
    steps_t = jnp.arange(NFFT, dtype=jnp.int32)
    freqs = jnp.arange(NF, dtype=jnp.int32)
    phase = (freqs[:, None] * steps_t[None, :] % NFFT).astype(jnp.float32) * (2.0 * math.pi / NFFT)
    hann = 0.5 - 0.5 * jnp.cos(steps_t.astype(jnp.float32) * (2.0 * math.pi / NFFT))
    factor = 1.0 / math.sqrt(3.0 * NFFT / 8.0)
    table = jnp.concatenate([jnp.cos(phase), -jnp.sin(phase)], axis=0) * hann[None, :] * factor
    return table.astype(jnp.bfloat16)

def reference(snapshots, weights):
    table = make_table().astype(jnp.float32)
    highest = lax.Precision.HIGHEST

    def accumulate(index, total):
        start = index * X_DEV
        block = lax.dynamic_slice_in_dim(snapshots, start, X_DEV, 2).astype(jnp.float32)
        scale = jnp.sqrt(lax.dynamic_slice_in_dim(weights, start, X_DEV, 0))
        coeffs = jnp.einsum('kt,btx->bkx', table, block, precision=highest) * scale[None, None, :]
        coeffs = coeffs.reshape(NB, 2, NF, X_DEV)
        real_part = jnp.einsum('acfx,bcfx->afb', coeffs, coeffs, precision=highest)
        imag_part = jnp.einsum('afx,bfx->afb', coeffs[:, 0], coeffs[:, 1], precision=highest) - jnp.einsum('afx,bfx->afb', coeffs[:, 1], coeffs[:, 0], precision=highest)
        return total + jnp.stack([real_part, imag_part], axis=2)
    start_total = jnp.zeros((NB, NF, 2, NB), jnp.float32)
    return lax.fori_loop(0, N_SPACE, accumulate, start_total)
```

```python
import functools
import math

import jax
import jax.numpy as jnp
import ml_dtypes
import numpy as np
from jax import lax
from jax.experimental import pallas as pl
from jax.experimental.pallas import tpu as pltpu
from jax.sharding import PartitionSpec as P

CHUNKS = 1
LANES = 256


def table_rows(length, owners, chunks):
    count = length // 2
    steps_t = np.arange(length, dtype=np.int32)
    freqs = np.arange(count, dtype=np.int32)
    phase = (freqs[:, None] * steps_t[None, :] % length).astype(np.float32) * np.float32(
        2.0 * math.pi / length
    )
    hann = np.float32(0.5) - np.float32(0.5) * np.cos(
        steps_t.astype(np.float32) * np.float32(2.0 * math.pi / length)
    )
    factor = np.float32(1.0 / math.sqrt(3.0 * length / 8.0))
    table = np.stack([np.cos(phase), -np.sin(phase)], axis=1) * hann[None, None, :] * factor
    table = table.astype(ml_dtypes.bfloat16)
    per = count // owners // chunks
    table = table.reshape(owners, chunks, per, 2, length).transpose(1, 0, 2, 3, 4)
    return table.reshape(chunks, owners * per * 2, length)


def transform_kernel(table_ref, weights_ref, block_ref, out_ref, rows_ref):
    blocks = block_ref.shape[0]
    rows = table_ref.shape[0]
    lanes = block_ref.shape[2]
    scale = jnp.sqrt(weights_ref[...])
    for b in range(blocks):
        coeffs = jnp.dot(table_ref[...], block_ref[b], preferred_element_type=jnp.float32)
        coeffs = coeffs * scale
        for i in range(lanes // 128):
            rows_ref[i, pl.ds(b, rows, stride=blocks), :] = coeffs[:, i * 128 : (i + 1) * 128]
    for i in range(lanes // 128):
        ordered = rows_ref[i].astype(jnp.bfloat16)
        out_ref[:, :, i * 128 : (i + 1) * 128] = ordered.reshape(rows, blocks, 128)


def transform(table, weights, snapshots):
    blocks, length, points = snapshots.shape
    rows = table.shape[0]
    return pl.pallas_call(
        transform_kernel,
        grid=(points // LANES,),
        in_specs=[
            pl.BlockSpec((rows, length), lambda i: (0, 0)),
            pl.BlockSpec((1, LANES), lambda i: (0, i)),
            pl.BlockSpec((blocks, length, LANES), lambda i: (0, 0, i)),
        ],
        out_specs=pl.BlockSpec((rows, blocks, LANES), lambda i: (0, 0, i)),
        out_shape=jax.ShapeDtypeStruct((rows, blocks, points), jnp.bfloat16),
        scratch_shapes=[pltpu.VMEM((LANES // 128, rows * blocks, 128), jnp.float32)],
        compiler_params=pltpu.CompilerParams(vmem_limit_bytes=48 * 1024 * 1024),
        cost_estimate=pl.CostEstimate(
            flops=2 * rows * length * blocks * points,
            bytes_accessed=2 * blocks * points * (length + rows),
            transcendentals=0,
        ),
        name="transform",
    )(table, weights.reshape(1, points), snapshots)


def cross_kernel(coeffs_ref, out_ref):
    owners, _, blocks, points = coeffs_ref.shape
    spaces = out_ref.shape[0]
    total = owners * blocks
    mine = total // spaces
    real = coeffs_ref[:, 0].reshape(total, points)
    imag = coeffs_ref[:, 1].reshape(total, points)
    across = (((1,), (1,)), ((), ()))
    first = lax.dot_general(
        real, jnp.concatenate([real, imag], axis=0), across, preferred_element_type=jnp.float32
    )
    second = lax.dot_general(
        imag, jnp.concatenate([imag, real], axis=0), across, preferred_element_type=jnp.float32
    )
    real_part = first[:, :total] + second[:, :total]
    imag_part = first[:, total:] - second[:, total:]
    for s in range(spaces):
        out_ref[s, 0, :mine, :] = real_part[s * mine : (s + 1) * mine]
        out_ref[s, 0, mine:, :] = imag_part[s * mine : (s + 1) * mine]


def cross(coeffs, spaces):
    owners, rows, blocks, points = coeffs.shape
    total = owners * blocks
    freqs = rows // 2
    return pl.pallas_call(
        cross_kernel,
        grid=(freqs,),
        in_specs=[pl.BlockSpec((owners, 2, blocks, points), lambda k: (0, k, 0, 0))],
        out_specs=pl.BlockSpec((spaces, 1, 2 * total // spaces, total), lambda k: (0, k, 0, 0)),
        out_shape=jax.ShapeDtypeStruct((spaces, freqs, 2 * total // spaces, total), jnp.float32),
        compiler_params=pltpu.CompilerParams(vmem_limit_bytes=48 * 1024 * 1024),
        cost_estimate=pl.CostEstimate(
            flops=8 * freqs * total * total * points,
            bytes_accessed=2 * rows * total * points + 8 * freqs * total * total,
            transcendentals=0,
        ),
        name="cross",
    )(coeffs)


def per_device(owners, spaces, snapshots, weights):
    blocks, length, points = snapshots.shape
    tables = table_rows(length, owners, CHUNKS)
    parts = []
    for c in range(CHUNKS):
        coeffs = transform(jnp.asarray(tables[c]), weights, snapshots)
        coeffs = coeffs.reshape(owners, -1, blocks, points)
        moved = lax.all_to_all(coeffs, "tm", split_axis=0, concat_axis=0, tiled=True)
        rows = cross(moved, spaces)
        rows = lax.all_to_all(rows, "space", split_axis=0, concat_axis=0, tiled=True)
        parts.append(jnp.sum(rows, axis=0))
    spectra = jnp.concatenate(parts, axis=0)
    freqs, both, total = spectra.shape
    return spectra.reshape(freqs, 2, both // 2, total).transpose(2, 0, 1, 3)


def solution(mesh):
    placed = (P("tm", None, "space"), P("space"))
    return jax.shard_map(
        functools.partial(per_device, mesh.shape["tm"], mesh.shape["space"]),
        mesh=mesh,
        in_specs=placed,
        out_specs=P("space", "tm", None, None),
        check_vma=False,
    )
```

```python
import functools
import math

import jax
import jax.numpy as jnp
import ml_dtypes
import numpy as np
from jax import lax
from jax.experimental import pallas as pl
from jax.experimental.pallas import tpu as pltpu
from jax.sharding import PartitionSpec as P

LANES = 512
PLANES = 2
MIB = 1024 * 1024


def make_table(length):
    count = length // 2
    steps_t = np.arange(length, dtype=np.int32)
    freqs = np.arange(count, dtype=np.int32)
    turn = np.float32(2.0 * math.pi / length)
    phase = (freqs[:, None] * steps_t[None, :] % length).astype(np.float32) * turn
    hann = np.float32(0.5) - np.float32(0.5) * np.cos(steps_t.astype(np.float32) * turn)
    factor = np.float32(1.0 / math.sqrt(3.0 * length / 8.0))
    table = np.stack([np.cos(phase), -np.sin(phase)], axis=1) * hann * factor
    return table.astype(ml_dtypes.bfloat16).reshape(2 * count, length)


def transform_kernel(table_ref, weights_ref, block_ref, out_ref, rows_ref):
    blocks = block_ref.shape[0]
    lanes = block_ref.shape[2]
    rows = table_ref.shape[0]
    stride = rows_ref.shape[1] // rows
    scale = jnp.sqrt(weights_ref[...])
    for b in range(blocks):
        coeffs = jnp.dot(table_ref[...], block_ref[b], preferred_element_type=jnp.float32)
        coeffs = coeffs * scale
        for i in range(lanes // 128):
            rows_ref[i, pl.ds(b, rows, stride=stride), :] = coeffs[:, i * 128 : (i + 1) * 128]
    for i in range(lanes // 128):
        for j in range(rows):
            ordered = rows_ref[i, j * stride : j * stride + blocks, :]
            out_ref[j, :, i * 128 : (i + 1) * 128] = ordered.astype(jnp.bfloat16)


def transform(table, weights, snapshots):
    blocks, length, points = snapshots.shape
    rows = table.shape[0]
    lanes = min(LANES, points)
    return pl.pallas_call(
        transform_kernel,
        grid=(points // lanes,),
        in_specs=[
            pl.BlockSpec((rows, length), lambda i: (0, 0)),
            pl.BlockSpec((1, lanes), lambda i: (0, i)),
            pl.BlockSpec((blocks, length, lanes), lambda i: (0, 0, i)),
        ],
        out_specs=pl.BlockSpec((rows, blocks, lanes), lambda i: (0, 0, i)),
        out_shape=jax.ShapeDtypeStruct((rows, blocks, points), jnp.bfloat16),
        scratch_shapes=[pltpu.VMEM((lanes // 128, rows * (blocks + 1), 128), jnp.float32)],
        compiler_params=pltpu.CompilerParams(vmem_limit_bytes=56 * MIB),
        cost_estimate=pl.CostEstimate(
            flops=2 * rows * length * blocks * points,
            bytes_accessed=2 * blocks * points * (length + rows),
            transcendentals=0,
        ),
        name="transform",
    )(table, weights.reshape(1, points), snapshots)


def cross_kernel(coeffs_ref, out_ref):
    owners, places, rows, blocks, points = coeffs_ref.shape
    spaces = out_ref.shape[0]
    total = owners * blocks
    mine = total // spaces
    for k in range(rows // 2):
        pieces = []
        for p in range(places):
            real = coeffs_ref[:, p, 2 * k].reshape(total, points)
            imag = coeffs_ref[:, p, 2 * k + 1].reshape(total, points)
            pieces.append(jnp.concatenate([real, imag], axis=0))
        both = jnp.concatenate(pieces, axis=1)
        grams = lax.dot_general(
            both, both, (((1,), (1,)), ((), ())), preferred_element_type=jnp.float32
        )
        real_part = grams[:total, :total] + grams[total:, total:]
        imag_part = grams[:total, total:] - grams[total:, :total]
        for s in range(spaces):
            out_ref[s, k, :mine, :] = real_part[s * mine : (s + 1) * mine]
            out_ref[s, k, mine:, :] = imag_part[s * mine : (s + 1) * mine]


def cross(coeffs, spaces):
    owners, places, rows, blocks, points = coeffs.shape
    total = owners * blocks
    freqs = rows // 2
    shape = (spaces, freqs, 2 * total // spaces, total)
    return pl.pallas_call(
        cross_kernel,
        in_specs=[pl.BlockSpec(memory_space=pltpu.VMEM)],
        out_specs=pl.BlockSpec(memory_space=pltpu.VMEM),
        out_shape=jax.ShapeDtypeStruct(shape, jnp.float32),
        compiler_params=pltpu.CompilerParams(vmem_limit_bytes=32 * MIB),
        cost_estimate=pl.CostEstimate(
            flops=8 * freqs * total * total * points * places,
            bytes_accessed=2 * rows * total * points * places + 8 * freqs * total * total,
            transcendentals=0,
        ),
        name="cross",
    )(coeffs)


def per_device(owners, spaces, snapshots, weights):
    blocks, length, points = snapshots.shape
    table = jnp.asarray(make_table(length))
    rest = spaces // 8
    places = PLANES * rest
    groups = [
        [t * spaces + z * rest + r for t in range(owners) for z in range(h, h + PLANES) for r in range(rest)]
        for h in range(0, spaces // rest, PLANES)
    ]
    coeffs = transform(table, weights, snapshots)
    coeffs = coeffs.reshape(owners * places, -1, blocks, points)
    moved = lax.all_to_all(
        coeffs, ("tm", "space"), split_axis=0, concat_axis=0, tiled=True, axis_index_groups=groups
    )
    sums = cross(moved.reshape(owners, places, -1, blocks, points), spaces)
    sums = lax.all_to_all(sums, "space", split_axis=0, concat_axis=0, tiled=True)
    freqs, both, total = sums.shape[1:]
    spectra = jnp.sum(sums.reshape(-1, places * freqs, both, total), axis=0)
    return spectra.reshape(places * freqs, 2, both // 2, total).transpose(2, 0, 1, 3)


def solution(mesh):
    placed = (P("tm", None, "space"), P("space"))
    return jax.shard_map(
        functools.partial(per_device, mesh.shape["tm"], mesh.shape["space"]),
        mesh=mesh,
        in_specs=placed,
        out_specs=P("space", "tm", None, None),
        check_vma=False,
    )
```

```python
import functools
import math

import jax
import jax.numpy as jnp
import numpy as np
from jax import lax
from jax.experimental import pallas as pl
from jax.experimental.pallas import tpu as pltpu
from jax.sharding import PartitionSpec as P

PARTS = 4
GROUPS = (2, 4, 4, 6)
AHEAD = 4
PLANES = 2
MIB = 1024 * 1024


def wave(steps, length):
    half = length // 2
    below = jnp.where(steps < half, steps, steps - half)
    angle = (half // 2 - below).astype(jnp.float32) * np.float32(2.0 * math.pi / length)
    square = angle * angle
    series = jnp.full_like(angle, np.float32(1.0 / math.factorial(13)))
    for n in (11, 9, 7, 5, 3, 1):
        sign = -1.0 if n % 4 == 3 else 1.0
        series = series * square + np.float32(sign / math.factorial(n))
    return jnp.where(steps < half, series * angle, -(series * angle))


def make_table(rows, length):
    row = lax.broadcasted_iota(jnp.int32, (rows, length), 0)
    step = lax.broadcasted_iota(jnp.int32, (rows, length), 1)
    turns = ((row >> 1) * step + (row & 1) * (length // 4)) & (length - 1)
    times = lax.broadcasted_iota(jnp.int32, (8, length), 1)
    hann = np.float32(0.5) - np.float32(0.5) * wave(times, length)
    factor = np.float32(1.0 / math.sqrt(3.0 * length / 8.0))
    table = wave(turns, length) * hann[:1] * factor
    return table.astype(jnp.bfloat16)


def transform_kernel(
    weights_ref, block_ref, out_ref, ready_ref, scale_ref, held_ref, rows_ref, sems
):
    blocks, length, points = block_ref.shape
    rows = ready_ref.shape[0]
    parts, tiles, spread, _ = rows_ref.shape
    stride = spread // rows
    lanes = points // parts
    second = pltpu.make_async_copy(weights_ref, scale_ref, sems.at[blocks])
    edges = np.cumsum((0,) + GROUPS)
    spans = [slice(int(a), int(b)) for a, b in zip(edges[:-1], edges[1:])]
    copies = [
        pltpu.make_async_copy(block_ref.at[span], held_ref.at[span], sems.at[g])
        for g, span in enumerate(spans)
    ]
    copies[0].start()
    second.start()
    for copy in copies[1:AHEAD]:
        copy.start()

    def reorder(h, start, stop):
        for j in range(start, stop):
            for i in range(tiles):
                ordered = rows_ref[h, i, j * stride : j * stride + blocks, :]
                lane = h * lanes + i * 128
                out_ref[j, :, lane : lane + 128] = ordered.astype(jnp.bfloat16)

    ready_ref[...] = make_table(rows, length)
    second.wait()
    scale_ref[...] = jnp.sqrt(scale_ref[...])

    def multiply(b, h):
        here = slice(h * lanes, (h + 1) * lanes)
        coeffs = jnp.dot(ready_ref[...], held_ref[b, :, here], preferred_element_type=jnp.float32)
        coeffs = coeffs * scale_ref[:, here]
        for i in range(tiles):
            rows_ref[h, i, pl.ds(b, rows, stride=stride), :] = coeffs[:, i * 128 : (i + 1) * 128]

    last = len(spans) - 1
    for g, span in enumerate(spans):
        copies[g].wait()
        if g + AHEAD <= last:
            copies[g + AHEAD].start()
        inside = range(span.start, span.stop)
        if g < last:
            for b in inside:
                for h in range(parts):
                    multiply(b, h)
        else:
            share = rows // len(inside)
            for h in range(parts):
                for n, b in enumerate(inside):
                    multiply(b, h)
                    if h > 0:
                        reorder(h - 1, n * share, (n + 1) * share if b + 1 < blocks else rows)
    reorder(parts - 1, 0, rows)


def transform(weights, snapshots):
    blocks, length, points = snapshots.shape
    rows = length
    tiles = points // PARTS // 128
    return pl.pallas_call(
        transform_kernel,
        in_specs=[pl.BlockSpec(memory_space=pl.ANY)] * 2,
        out_specs=pl.BlockSpec(memory_space=pltpu.VMEM),
        out_shape=jax.ShapeDtypeStruct((rows, blocks, points), jnp.bfloat16),
        scratch_shapes=[
            pltpu.VMEM((rows, length), jnp.bfloat16),
            pltpu.VMEM((1, points), jnp.float32),
            pltpu.VMEM((blocks, length, points), jnp.bfloat16),
            pltpu.VMEM((PARTS, tiles, rows * (blocks + 1), 128), jnp.float32),
            pltpu.SemaphoreType.DMA((blocks + 1,)),
        ],
        compiler_params=pltpu.CompilerParams(vmem_limit_bytes=40 * MIB),
        cost_estimate=pl.CostEstimate(
            flops=2 * rows * length * blocks * points,
            bytes_accessed=2 * blocks * points * (length + rows),
            transcendentals=0,
        ),
        name="transform",
    )(weights.reshape(1, points), snapshots)


def cross_kernel(coeffs_ref, out_ref):
    owners, places, rows, blocks, points = coeffs_ref.shape
    spaces = out_ref.shape[0]
    total = owners * blocks
    mine = total // spaces
    for k in range(rows // 2):
        pieces = []
        for p in range(places):
            real = coeffs_ref[:, p, 2 * k].reshape(total, points)
            imag = coeffs_ref[:, p, 2 * k + 1].reshape(total, points)
            pieces.append(jnp.concatenate([real, imag], axis=0))
        both = jnp.concatenate(pieces, axis=1)
        grams = lax.dot_general(
            both, both, (((1,), (1,)), ((), ())), preferred_element_type=jnp.float32
        )
        real_part = grams[:total, :total] + grams[total:, total:]
        imag_part = grams[:total, total:] - grams[total:, :total]
        for s in range(spaces):
            out_ref[s, k, :mine, :] = real_part[s * mine : (s + 1) * mine]
            out_ref[s, k, mine:, :] = imag_part[s * mine : (s + 1) * mine]


def cross(coeffs, spaces):
    owners, places, rows, blocks, points = coeffs.shape
    total = owners * blocks
    freqs = rows // 2
    shape = (spaces, freqs, 2 * total // spaces, total)
    return pl.pallas_call(
        cross_kernel,
        in_specs=[pl.BlockSpec(memory_space=pltpu.VMEM)],
        out_specs=pl.BlockSpec(memory_space=pltpu.VMEM),
        out_shape=jax.ShapeDtypeStruct(shape, jnp.float32),
        compiler_params=pltpu.CompilerParams(vmem_limit_bytes=32 * MIB),
        cost_estimate=pl.CostEstimate(
            flops=8 * freqs * total * total * points * places,
            bytes_accessed=2 * rows * total * points * places + 8 * freqs * total * total,
            transcendentals=0,
        ),
        name="cross",
    )(coeffs)


def per_device(owners, spaces, snapshots, weights):
    blocks, _, points = snapshots.shape
    rest = spaces // 8
    places = PLANES * rest
    groups = [
        [t * spaces + z * rest + r for t in range(owners) for z in range(h, h + PLANES) for r in range(rest)]
        for h in range(0, spaces // rest, PLANES)
    ]
    coeffs = transform(weights, snapshots)
    coeffs = coeffs.reshape(owners * places, -1, blocks, points)
    moved = lax.all_to_all(
        coeffs, ("tm", "space"), split_axis=0, concat_axis=0, tiled=True, axis_index_groups=groups
    )
    sums = cross(moved.reshape(owners, places, -1, blocks, points), spaces)
    sums = lax.all_to_all(sums, "space", split_axis=0, concat_axis=0, tiled=True)
    freqs, both, total = sums.shape[1:]
    spectra = jnp.sum(sums.reshape(-1, places * freqs, both, total), axis=0)
    return spectra.reshape(places * freqs, 2, both // 2, total).transpose(2, 0, 1, 3)


def solution(mesh):
    placed = (P("tm", None, "space"), P("space"))
    return jax.shard_map(
        functools.partial(per_device, mesh.shape["tm"], mesh.shape["space"]),
        mesh=mesh,
        in_specs=placed,
        out_specs=P("space", "tm", None, None),
        check_vma=False,
    )
```

```python
import functools
import math

import jax
import jax.numpy as jnp
import numpy as np
from jax import lax
from jax.experimental import pallas as pl
from jax.experimental.pallas import tpu as pltpu
from jax.sharding import PartitionSpec as P

PARTS = 4
GROUPS = (2, 4, 4, 6)
AHEAD = 4
PLANES = 2
MIB = 1024 * 1024


def wave(steps, length):
    half = length // 2
    below = jnp.where(steps < half, steps, steps - half)
    angle = (half // 2 - below).astype(jnp.float32) * np.float32(2.0 * math.pi / length)
    square = angle * angle
    series = jnp.full_like(angle, np.float32(1.0 / math.factorial(13)))
    for n in (11, 9, 7, 5, 3, 1):
        sign = -1.0 if n % 4 == 3 else 1.0
        series = series * square + np.float32(sign / math.factorial(n))
    return jnp.where(steps < half, series * angle, -(series * angle))


def make_table(rows, length):
    row = lax.broadcasted_iota(jnp.int32, (rows, length), 0)
    step = lax.broadcasted_iota(jnp.int32, (rows, length), 1)
    turns = ((row >> 1) * step + (row & 1) * (length // 4)) & (length - 1)
    times = lax.broadcasted_iota(jnp.int32, (8, length), 1)
    hann = np.float32(0.5) - np.float32(0.5) * wave(times, length)
    factor = np.float32(1.0 / math.sqrt(3.0 * length / 8.0))
    table = wave(turns, length) * hann[:1] * factor
    return table.astype(jnp.bfloat16)


def transform_kernel(
    weights_ref, block_ref, out_ref, ready_ref, scale_ref, held_ref, rows_ref, sems
):
    blocks, length, points = block_ref.shape
    rows = ready_ref.shape[0]
    parts, tiles, spread, _ = rows_ref.shape
    stride = spread // rows
    lanes = points // parts
    second = pltpu.make_async_copy(weights_ref, scale_ref, sems.at[blocks])
    edges = np.cumsum((0,) + GROUPS)
    spans = [slice(int(a), int(b)) for a, b in zip(edges[:-1], edges[1:])]
    copies = [
        pltpu.make_async_copy(block_ref.at[span], held_ref.at[span], sems.at[g])
        for g, span in enumerate(spans)
    ]
    copies[0].start()
    second.start()
    for copy in copies[1:AHEAD]:
        copy.start()

    def reorder(h, start, stop):
        for j in range(start, stop):
            for i in range(tiles):
                ordered = rows_ref[h, i, j * stride : j * stride + blocks, :]
                lane = h * lanes + i * 128
                out_ref[j, :, lane : lane + 128] = ordered.astype(jnp.bfloat16)

    ready_ref[...] = make_table(rows, length)
    second.wait()
    scale_ref[...] = jnp.sqrt(scale_ref[...])

    def multiply(b, h):
        here = slice(h * lanes, (h + 1) * lanes)
        coeffs = jnp.dot(ready_ref[...], held_ref[b, :, here], preferred_element_type=jnp.float32)
        coeffs = coeffs * scale_ref[:, here]
        for i in range(tiles):
            rows_ref[h, i, pl.ds(b, rows, stride=stride), :] = coeffs[:, i * 128 : (i + 1) * 128]

    last = len(spans) - 1
    for g, span in enumerate(spans):
        copies[g].wait()
        if g + AHEAD <= last:
            copies[g + AHEAD].start()
        inside = range(span.start, span.stop)
        if g < last:
            for b in inside:
                for h in range(parts):
                    multiply(b, h)
        else:
            share = rows // len(inside)
            for h in range(parts):
                for n, b in enumerate(inside):
                    multiply(b, h)
                    if h > 0:
                        reorder(h - 1, n * share, (n + 1) * share if b + 1 < blocks else rows)
    reorder(parts - 1, 0, rows)


def transform(weights, snapshots):
    blocks, length, points = snapshots.shape
    rows = length
    tiles = points // PARTS // 128
    return pl.pallas_call(
        transform_kernel,
        in_specs=[pl.BlockSpec(memory_space=pl.ANY)] * 2,
        out_specs=pl.BlockSpec(memory_space=pltpu.VMEM),
        out_shape=jax.ShapeDtypeStruct((rows, blocks, points), jnp.bfloat16),
        scratch_shapes=[
            pltpu.VMEM((rows, length), jnp.bfloat16),
            pltpu.VMEM((1, points), jnp.float32),
            pltpu.VMEM((blocks, length, points), jnp.bfloat16),
            pltpu.VMEM((PARTS, tiles, rows * (blocks + 1), 128), jnp.float32),
            pltpu.SemaphoreType.DMA((blocks + 1,)),
        ],
        compiler_params=pltpu.CompilerParams(vmem_limit_bytes=40 * MIB),
        cost_estimate=pl.CostEstimate(
            flops=2 * rows * length * blocks * points,
            bytes_accessed=2 * blocks * points * (length + rows),
            transcendentals=0,
        ),
        name="transform",
    )(weights.reshape(1, points), snapshots)


def cross_kernel(coeffs_ref, out_ref):
    owners, places, rows, blocks, points = coeffs_ref.shape
    spaces = out_ref.shape[0]
    total = owners * blocks
    mine = total // spaces
    for k in range(rows // 2):
        pieces = []
        for p in range(places):
            real = coeffs_ref[:, p, 2 * k].reshape(total, points)
            imag = coeffs_ref[:, p, 2 * k + 1].reshape(total, points)
            pieces.append(jnp.concatenate([real, imag], axis=0))
        both = jnp.concatenate(pieces, axis=1)
        grams = lax.dot_general(
            both, both, (((1,), (1,)), ((), ())), preferred_element_type=jnp.float32
        )
        real_part = grams[:total, :total] + grams[total:, total:]
        imag_part = grams[:total, total:] - grams[total:, :total]
        for s in range(spaces):
            out_ref[s, k, :mine, :] = real_part[s * mine : (s + 1) * mine]
            out_ref[s, k, mine:, :] = imag_part[s * mine : (s + 1) * mine]


def cross(coeffs, spaces):
    owners, places, rows, blocks, points = coeffs.shape
    total = owners * blocks
    freqs = rows // 2
    shape = (spaces, freqs, 2 * total // spaces, total)
    return pl.pallas_call(
        cross_kernel,
        in_specs=[pl.BlockSpec(memory_space=pltpu.VMEM)],
        out_specs=pl.BlockSpec(memory_space=pltpu.VMEM),
        out_shape=jax.ShapeDtypeStruct(shape, jnp.float32),
        compiler_params=pltpu.CompilerParams(vmem_limit_bytes=32 * MIB),
        cost_estimate=pl.CostEstimate(
            flops=8 * freqs * total * total * points * places,
            bytes_accessed=2 * rows * total * points * places + 8 * freqs * total * total,
            transcendentals=0,
        ),
        name="cross",
    )(coeffs)


def gather_kernel(sums_ref, out_ref):
    total = sums_ref[0]
    for n in range(1, sums_ref.shape[0]):
        total = total + sums_ref[n]
    mine = out_ref.shape[0]
    for a in range(mine):
        for part in range(2):
            out_ref[a, :, part, :] = total[:, part * mine + a, :]


def gather(sums):
    _, freqs, both, total = sums.shape
    return pl.pallas_call(
        gather_kernel,
        in_specs=[pl.BlockSpec(memory_space=pltpu.VMEM)],
        out_specs=pl.BlockSpec(memory_space=pltpu.VMEM),
        out_shape=jax.ShapeDtypeStruct((both // 2, freqs, 2, total), jnp.float32),
        compiler_params=pltpu.CompilerParams(vmem_limit_bytes=8 * MIB),
        name="gather",
    )(sums)


def per_device(owners, spaces, snapshots, weights):
    blocks, _, points = snapshots.shape
    rest = spaces // 8
    places = PLANES * rest
    groups = [
        [t * spaces + z * rest + r for t in range(owners) for z in range(h, h + PLANES) for r in range(rest)]
        for h in range(0, spaces // rest, PLANES)
    ]
    coeffs = transform(weights, snapshots)
    coeffs = coeffs.reshape(owners * places, -1, blocks, points)
    moved = lax.all_to_all(
        coeffs, ("tm", "space"), split_axis=0, concat_axis=0, tiled=True, axis_index_groups=groups
    )
    sums = cross(moved.reshape(owners, places, -1, blocks, points), spaces)
    sums = lax.all_to_all(sums, "space", split_axis=0, concat_axis=0, tiled=True)
    freqs, both, total = sums.shape[1:]
    return gather(sums.reshape(-1, places * freqs, both, total))


def solution(mesh):
    placed = (P("tm", None, "space"), P("space"))
    return jax.shard_map(
        functools.partial(per_device, mesh.shape["tm"], mesh.shape["space"]),
        mesh=mesh,
        in_specs=placed,
        out_specs=P("space", "tm", None, None),
        check_vma=False,
    )
```

```python
import functools
import math

import jax
import jax.numpy as jnp
import numpy as np
from jax import lax
from jax.experimental import pallas as pl
from jax.experimental.pallas import tpu as pltpu
from jax.sharding import PartitionSpec as P

PARTS = 4
GROUPS = (1, 2, 3, 4, 6)
AHEAD = 5
PLANES = 2
MIB = 1024 * 1024


def wave(steps, length):
    half = length // 2
    below = jnp.where(steps < half, steps, steps - half)
    angle = (half // 2 - below).astype(jnp.float32) * np.float32(2.0 * math.pi / length)
    square = angle * angle
    series = jnp.full_like(angle, np.float32(1.0 / math.factorial(13)))
    for n in (11, 9, 7, 5, 3, 1):
        sign = -1.0 if n % 4 == 3 else 1.0
        series = series * square + np.float32(sign / math.factorial(n))
    return jnp.where(steps < half, series * angle, -(series * angle))


def make_table(rows, length):
    row = lax.broadcasted_iota(jnp.int32, (rows, length), 0)
    step = lax.broadcasted_iota(jnp.int32, (rows, length), 1)
    turns = ((row >> 1) * step + (row & 1) * (length // 4)) & (length - 1)
    times = lax.broadcasted_iota(jnp.int32, (8, length), 1)
    hann = np.float32(0.5) - np.float32(0.5) * wave(times, length)
    factor = np.float32(1.0 / math.sqrt(3.0 * length / 8.0))
    table = wave(turns, length) * hann[:1] * factor
    return table.astype(jnp.bfloat16)


def transform_kernel(
    weights_ref, block_ref, out_ref, ready_ref, scale_ref, held_ref, rows_ref, sems
):
    blocks, length, points = block_ref.shape
    rows = ready_ref.shape[0]
    parts, tiles, spread, _ = rows_ref.shape
    stride = spread // rows
    lanes = points // parts
    second = pltpu.make_async_copy(weights_ref, scale_ref, sems.at[blocks])
    edges = np.cumsum((0,) + GROUPS)
    spans = [slice(int(a), int(b)) for a, b in zip(edges[:-1], edges[1:])]
    copies = [
        pltpu.make_async_copy(block_ref.at[span], held_ref.at[span], sems.at[g])
        for g, span in enumerate(spans)
    ]
    copies[0].start()
    second.start()
    for copy in copies[1:AHEAD]:
        copy.start()

    def reorder(h, start, stop):
        for j in range(start, stop):
            for i in range(tiles):
                ordered = rows_ref[h, i, j * stride : j * stride + blocks, :]
                lane = h * lanes + i * 128
                out_ref[j, :, lane : lane + 128] = ordered.astype(jnp.bfloat16)

    ready_ref[...] = make_table(rows, length)
    second.wait()
    scale_ref[...] = jnp.sqrt(scale_ref[...])

    def multiply(b, h):
        here = slice(h * lanes, (h + 1) * lanes)
        coeffs = jnp.dot(ready_ref[...], held_ref[b, :, here], preferred_element_type=jnp.float32)
        coeffs = coeffs * scale_ref[:, here]
        for i in range(tiles):
            rows_ref[h, i, pl.ds(b, rows, stride=stride), :] = coeffs[:, i * 128 : (i + 1) * 128]

    last = len(spans) - 1
    for g, span in enumerate(spans):
        copies[g].wait()
        if g + AHEAD <= last:
            copies[g + AHEAD].start()
        inside = range(span.start, span.stop)
        if g < last:
            for b in inside:
                for h in range(parts):
                    multiply(b, h)
        else:
            share = rows // len(inside)
            for h in range(parts):
                for n, b in enumerate(inside):
                    multiply(b, h)
                    if h > 0:
                        reorder(h - 1, n * share, (n + 1) * share if b + 1 < blocks else rows)
    reorder(parts - 1, 0, rows)


def transform(weights, snapshots):
    blocks, length, points = snapshots.shape
    rows = length
    tiles = points // PARTS // 128
    return pl.pallas_call(
        transform_kernel,
        in_specs=[pl.BlockSpec(memory_space=pl.ANY)] * 2,
        out_specs=pl.BlockSpec(memory_space=pltpu.VMEM),
        out_shape=jax.ShapeDtypeStruct((rows, blocks, points), jnp.bfloat16),
        scratch_shapes=[
            pltpu.VMEM((rows, length), jnp.bfloat16),
            pltpu.VMEM((1, points), jnp.float32),
            pltpu.VMEM((blocks, length, points), jnp.bfloat16),
            pltpu.VMEM((PARTS, tiles, rows * (blocks + 1), 128), jnp.float32),
            pltpu.SemaphoreType.DMA((blocks + 1,)),
        ],
        compiler_params=pltpu.CompilerParams(vmem_limit_bytes=40 * MIB),
        cost_estimate=pl.CostEstimate(
            flops=2 * rows * length * blocks * points,
            bytes_accessed=2 * blocks * points * (length + rows),
            transcendentals=0,
        ),
        name="transform",
    )(weights.reshape(1, points), snapshots)


def cross_kernel(coeffs_ref, out_ref):
    owners, places, rows, blocks, points = coeffs_ref.shape
    spaces = out_ref.shape[0]
    total = owners * blocks
    mine = total // spaces
    for k in range(rows // 2):
        pieces = []
        for p in range(places):
            real = coeffs_ref[:, p, 2 * k].reshape(total, points)
            imag = coeffs_ref[:, p, 2 * k + 1].reshape(total, points)
            pieces.append(jnp.concatenate([real, imag], axis=0))
        both = jnp.concatenate(pieces, axis=1)
        grams = lax.dot_general(
            both, both, (((1,), (1,)), ((), ())), preferred_element_type=jnp.float32
        )
        real_part = grams[:total, :total] + grams[total:, total:]
        imag_part = grams[:total, total:] - grams[total:, :total]
        for s in range(spaces):
            out_ref[s, k, :mine, :] = real_part[s * mine : (s + 1) * mine]
            out_ref[s, k, mine:, :] = imag_part[s * mine : (s + 1) * mine]


def cross(coeffs, spaces):
    owners, places, rows, blocks, points = coeffs.shape
    total = owners * blocks
    freqs = rows // 2
    shape = (spaces, freqs, 2 * total // spaces, total)
    return pl.pallas_call(
        cross_kernel,
        in_specs=[pl.BlockSpec(memory_space=pltpu.VMEM)],
        out_specs=pl.BlockSpec(memory_space=pltpu.VMEM),
        out_shape=jax.ShapeDtypeStruct(shape, jnp.float32),
        compiler_params=pltpu.CompilerParams(vmem_limit_bytes=32 * MIB),
        cost_estimate=pl.CostEstimate(
            flops=8 * freqs * total * total * points * places,
            bytes_accessed=2 * rows * total * points * places + 8 * freqs * total * total,
            transcendentals=0,
        ),
        name="cross",
    )(coeffs)


def gather_kernel(sums_ref, out_ref):
    total = sums_ref[0]
    for n in range(1, sums_ref.shape[0]):
        total = total + sums_ref[n]
    mine = out_ref.shape[0]
    for a in range(mine):
        for part in range(2):
            out_ref[a, :, part, :] = total[:, part * mine + a, :]


def gather(sums):
    _, freqs, both, total = sums.shape
    return pl.pallas_call(
        gather_kernel,
        in_specs=[pl.BlockSpec(memory_space=pltpu.VMEM)],
        out_specs=pl.BlockSpec(memory_space=pltpu.VMEM),
        out_shape=jax.ShapeDtypeStruct((both // 2, freqs, 2, total), jnp.float32),
        compiler_params=pltpu.CompilerParams(vmem_limit_bytes=8 * MIB),
        name="gather",
    )(sums)


def per_device(owners, spaces, snapshots, weights):
    blocks, _, points = snapshots.shape
    rest = spaces // 8
    places = PLANES * rest
    groups = [
        [t * spaces + z * rest + r for t in range(owners) for z in range(h, h + PLANES) for r in range(rest)]
        for h in range(0, spaces // rest, PLANES)
    ]
    coeffs = transform(weights, snapshots)
    coeffs = coeffs.reshape(owners * places, -1, blocks, points)
    moved = lax.all_to_all(
        coeffs, ("tm", "space"), split_axis=0, concat_axis=0, tiled=True, axis_index_groups=groups
    )
    sums = cross(moved.reshape(owners, places, -1, blocks, points), spaces)
    sums = lax.all_to_all(sums, "space", split_axis=0, concat_axis=0, tiled=True)
    freqs, both, total = sums.shape[1:]
    return gather(sums.reshape(-1, places * freqs, both, total))


def solution(mesh):
    placed = (P("tm", None, "space"), P("space"))
    return jax.shard_map(
        functools.partial(per_device, mesh.shape["tm"], mesh.shape["space"]),
        mesh=mesh,
        in_specs=placed,
        out_specs=P("space", "tm", None, None),
        check_vma=False,
    )
```
